512 devices in a mesh: az: 64 (over x, z), rad: 4 (over y_lo, core), ax: 2 (over y_hi).
Axes of the slice: x: 4, y: 4 (y_hi: 2, y_lo: 2; y = y_hi * 2 + y_lo), z: 16, core: 2. Of those that a mesh axis runs over, the one named last changes fastest.
Arguments:
- state: bfloat16 [2, 6, 32, 1536, 512], P('ax', None, None, 'az', 'rad'), may hold values from -6 to 6
- diffusivity: bfloat16 [2, 32, 1536, 512], P('ax', None, 'az', 'rad'), may hold values from 0.019897461 to 0.15917969
- rotor_step: int32 [1], replicated, may hold values from 0 to 1535
Outputs:
- next_state: bfloat16 [2, 6, 32, 1536, 512], P('ax', None, None, 'az', 'rad')
The draws below stay inside these ranges and needn't reach their ends.
All inputs are finite; a program needn't handle non-finite values.
Results may differ from the reference program's by a relative error of at most 0.006.
Values may be sent and summed in bfloat16 or wider, within the bound.
A program may use at most 64 MiB of HBM per device.

```python
import math
import jax
import jax.numpy as jnp
from jax import lax

FIELDS = 6
CYCLE = 1536
MODES = 512
PLANES = 32
RADII = 512


def levels(key, extent, pieces, smallest, largest):
    factor_of, own = 1.0, jax.random.fold_in(key, 6)
    for dim, parts in pieces:
        heights = jnp.exp(jax.random.uniform(jax.random.fold_in(own, dim), (parts,), jnp.float32, smallest / len(pieces), largest / len(pieces)))
        factor_of = factor_of * jnp.repeat(heights, extent[dim] // parts).reshape([-1 if axis == dim else 1 for axis in range(len(extent))])
    return factor_of


def scatter_about(stream_key, dims, scale, reach, shards=(), kind=jnp.bfloat16):
    gain = levels(stream_key, dims, shards, -0.22, 0.18) if shards else 1.0
    result = jax.random.normal(stream_key, dims, jnp.float32) * scale * gain
    return jnp.minimum(jnp.maximum(result, -reach), reach).astype(kind)


def setup_inputs(seed: int = 0) -> dict:
    arg_keys = jax.random.split(jax.random.key(seed), 4)
    state = scatter_about(arg_keys[0], (2, FIELDS, PLANES, CYCLE, RADII), 1.0, 6.0, ((0, 2), (3, 64), (4, 4)))
    diffusivity = jnp.clip(jnp.exp(math.log(0.15917969) - 2.0794415 * jax.random.uniform(arg_keys[1], (2, PLANES, CYCLE, RADII), jnp.float32) ** levels(arg_keys[1], (2, PLANES, CYCLE, RADII), ((0, 2), (2, 64), (3, 4)), -0.2, 0.2)), 0.019897461, 0.15917969).astype(jnp.bfloat16)
    rotor_step = jax.random.randint(arg_keys[2], (1,), 0, CYCLE).astype(jnp.int32)
    return {"state": state, "diffusivity": diffusivity, "rotor_step": rotor_step}


def angle_grid(first_count, second_count, cycle_cells):
    first_index = jnp.arange(first_count, dtype=jnp.int32)
    second_index = jnp.arange(second_count, dtype=jnp.int32)
    product_mod = jnp.mod(first_index[:, None] * second_index[None, :], cycle_cells)
    return product_mod.astype(jnp.float32) * (2.0 * math.pi / cycle_cells)


def forward_table(cycle_cells, mode_count):
    angles = angle_grid(cycle_cells, mode_count, cycle_cells)
    return jnp.concatenate([jnp.cos(angles), jnp.sin(angles)], axis=1).astype(jnp.bfloat16)


def inverse_table(cycle_cells, mode_count):
    angles = angle_grid(mode_count, cycle_cells, cycle_cells)
    mode_index = jnp.arange(mode_count, dtype=jnp.int32)
    weights = (jnp.where(mode_index == 0, 1.0, 2.0).astype(jnp.float32) / cycle_cells)[:, None]
    return jnp.concatenate([weights * jnp.cos(angles), weights * jnp.sin(angles)], axis=0).astype(jnp.bfloat16)


def rotate_modes(spectra, mode_count, cycle_cells, cell_shift):
    mode_index = jnp.arange(mode_count, dtype=jnp.int32)
    turned = jnp.mod(mode_index * cell_shift, cycle_cells).astype(jnp.float32) * (2.0 * math.pi / cycle_cells)
    cos_part = jnp.cos(turned)[None, :, None]
    sin_part = jnp.sin(turned)[None, :, None]
    cosine_part = spectra[:, :mode_count, :]
    sine_part = spectra[:, mode_count:, :]
    return jnp.concatenate([cosine_part * cos_part - sine_part * sin_part,
                            cosine_part * sin_part + sine_part * cos_part], axis=1).astype(jnp.bfloat16)


def carry_cycles(cycle_block, cycle_table, back_table, cell_shift):
    spectra = jnp.einsum("ar,ak->kr", cycle_block.astype(jnp.float32), cycle_table.astype(jnp.float32),
                         precision=lax.Precision.HIGHEST)
    spun = rotate_modes(spectra[None], MODES, CYCLE, cell_shift)[0]
    rebuilt = jnp.einsum("kr,ka->ar", spun.astype(jnp.float32), back_table.astype(jnp.float32),
                         precision=lax.Precision.HIGHEST)
    return rebuilt.astype(jnp.bfloat16)


def settle(field_block, coeffs, carried, weight):
    values = field_block.astype(jnp.float32)
    value_pad = jnp.pad(values, ((1, 1), (0, 0), (1, 1)))
    coeff_pad = jnp.pad(coeffs, ((1, 1), (0, 0), (1, 1)))
    neighbours = [
        (jnp.roll(values, -1, axis=1), jnp.roll(coeffs, -1, axis=1)),
        (jnp.roll(values, 1, axis=1), jnp.roll(coeffs, 1, axis=1)),
        (value_pad[2:, :, 1:-1], coeff_pad[2:, :, 1:-1]),
        (value_pad[:-2, :, 1:-1], coeff_pad[:-2, :, 1:-1]),
        (value_pad[1:-1, :, 2:], coeff_pad[1:-1, :, 2:]),
        (value_pad[1:-1, :, :-2], coeff_pad[1:-1, :, :-2]),
    ]
    flux_sum = jnp.zeros_like(values)
    for near_value, near_coeff in neighbours:
        flux_sum = flux_sum + 0.5 * (coeffs + near_coeff) * (near_value - values)
    blended = values + flux_sum + weight[:, None, None] * (carried.astype(jnp.float32) - values)
    return blended.astype(jnp.bfloat16)


def reference(state, diffusivity, rotor_step):
    cycle_table = forward_table(CYCLE, MODES)
    back_table = inverse_table(CYCLE, MODES)
    carried_sides = []
    for sender in range(2):
        cell_shift = (1 - 2 * sender) * rotor_step[0]
        cycle_rows = state[sender].reshape(FIELDS * PLANES, CYCLE, RADII)
        moved = lax.map(lambda cycle_block: carry_cycles(cycle_block, cycle_table, back_table, cell_shift), cycle_rows)
        carried_sides.append(moved.reshape(FIELDS, PLANES, CYCLE, RADII))
    outputs = []
    for side_index in range(2):
        carried = carried_sides[1 - side_index]
        plane_mid = (jnp.arange(PLANES, dtype=jnp.float32) + 0.5) / PLANES
        weight = plane_mid if side_index == 0 else 1.0 - plane_mid
        coeffs = diffusivity[side_index].astype(jnp.float32)
        settled = lax.map(lambda pair: settle(pair[0], coeffs, pair[1], weight), (state[side_index], carried))
        outputs.append(settled)
    return jnp.stack(outputs, axis=0)
```

```python
import math

import jax
import jax.numpy as jnp
from jax import lax
from jax.experimental import pallas as pl
from jax.experimental.pallas import tpu as pltpu
from jax.sharding import PartitionSpec as P

CYCLE = 1536
MODES = 512
FIELDS = 6
PLANES = 32
ROWS = FIELDS * PLANES
CELLS = 24
LANES = 128
RING = 64
COLS = 16
PARTS = 3
GROUP = 8
MESH = pl.DeviceIdType.MESH
F32 = jnp.float32
BF16 = jnp.bfloat16


def iota(shape, dim):
    return lax.broadcasted_iota(jnp.int32, shape, dim)


def wrapped(product):
    left = product - jnp.floor(product * (1.0 / CYCLE)) * float(CYCLE)
    left = jnp.where(left < 0.0, left + float(CYCLE), left)
    return jnp.where(left >= float(CYCLE), left - float(CYCLE), left)


def cos_sin(cells):
    quarter = jnp.floor(cells * (4.0 / CYCLE) + 0.5)
    t = (cells - quarter * (CYCLE / 4.0)) * (2.0 * math.pi / CYCLE)
    u = t * t
    sine = t * (1.0 + u * (-1.0 / 6 + u * (1.0 / 120 + u * (-1.0 / 5040 + u * (1.0 / 362880)))))
    cosine = 1.0 + u * (-0.5 + u * (1.0 / 24 + u * (-1.0 / 720 + u * (1.0 / 40320 - u * (1.0 / 3628800)))))
    odd = (quarter == 1.0) | (quarter == 3.0)
    c = jnp.where(odd, sine, cosine)
    s = jnp.where(odd, cosine, sine)
    c = jnp.where((quarter == 1.0) | (quarter == 2.0), -c, c)
    s = jnp.where((quarter == 2.0) | (quarter == 3.0), -s, s)
    return c, s


def kernel(
    state,
    diffusivity,
    rotor_step,
    out,
    cycles,
    rebuilt,
    carried,
    base,
    forward,
    back,
    spun,
    phase,
    fine,
    coarse,
    edge_rows,
    near_rows,
    near_rows32,
    edge_cols,
    near_cols,
    near_cols_t,
    face_x,
    face,
    send1,
    recv1,
    send2,
    recv2,
    send_h,
    recv_h,
):
    az, rad, ax = lax.axis_index("az"), lax.axis_index("rad"), lax.axis_index("ax")
    x, z = az // COLS, lax.rem(az, COLS)
    az_up, az_down = lax.rem(az + 1, RING), lax.rem(az + RING - 1, RING)
    rad_up, rad_down = lax.rem(rad + 1, 4), lax.rem(rad + 3, 4)

    def partner(k):
        m = k // 4
        far = (m + 1) // 2
        dz = jnp.where(lax.rem(m, 2) == 1, far, COLS - far)
        return lax.rem(x + lax.rem(k, 4), 4) * COLS + lax.rem(z + dz, COLS)

    barrier = pltpu.get_barrier_semaphore()

    def greet(k, carry):
        pl.semaphore_signal(barrier, inc=1, device_id=(partner(k), rad, 1 - ax), device_id_type=MESH)

        @pl.when(k > 0)
        def _():
            pl.semaphore_signal(barrier, inc=1, device_id=(partner(k), rad, ax), device_id_type=MESH)

        return carry

    lax.fori_loop(0, RING, greet, 0)
    pl.semaphore_signal(barrier, inc=1, device_id=(az, rad_up, ax), device_id_type=MESH)
    pl.semaphore_signal(barrier, inc=1, device_id=(az, rad_down, ax), device_id_type=MESH)
    pl.semaphore_wait(barrier, 2 * RING + 1)

    for part in range(PARTS):

        def send(k, carry, part=part):
            j = partner(k)
            pltpu.make_async_remote_copy(
                src_ref=state.at[part * RING + j],
                dst_ref=cycles.at[part, az],
                send_sem=send1.at[part],
                recv_sem=recv1.at[part],
                device_id=(j, rad, 1 - ax),
                device_id_type=MESH,
            ).start()
            return carry

        lax.fori_loop(0, RING, send, 0)

    def edges(ref, i, slot, acc):
        block = ref[pl.ds(pl.multiple_of(i * 16, 16), 16)]
        wide = block.astype(F32)
        rows = pl.ds(pl.multiple_of(slot * 16, 16), 16)
        edge_rows[0, rows, :] = wide[:, 0, :].astype(BF16)
        edge_rows[1, rows, :] = wide[:, CELLS - 1, :].astype(BF16)
        row, lane = iota((32, LANES), 0), iota((32, LANES), 1)
        pick = ((row == slot) & (lane == 0)) | ((row == slot + 16) & (lane == LANES - 1))
        return acc + lax.dot_general(
            jnp.where(pick, 1.0, 0.0).astype(BF16),
            block.reshape(16 * CELLS, LANES),
            (((1,), (1,)), ((), ())),
            preferred_element_type=F32,
        )

    acc = jnp.zeros((32, 16 * CELLS), F32)
    acc = lax.fori_loop(0, ROWS // 16, lambda i, a: edges(state, i, i, a), acc)
    acc = lax.fori_loop(0, PLANES // 16, lambda i, a: edges(diffusivity, i, i + ROWS // 16, a), acc)
    edge_cols[0] = acc[:16].astype(BF16)
    edge_cols[1] = acc[16:].astype(BF16)

    def halo(n, src, dst, target):
        return pltpu.make_async_remote_copy(
            src_ref=src, dst_ref=dst, send_sem=send_h.at[n], recv_sem=recv_h.at[n],
            device_id=target, device_id_type=MESH,
        )

    halos = [
        halo(0, edge_rows.at[1], near_rows.at[0], (az_up, rad, ax)),
        halo(1, edge_rows.at[0], near_rows.at[1], (az_down, rad, ax)),
        halo(2, edge_cols.at[1], near_cols.at[0], (az, rad_up, ax)),
        halo(3, edge_cols.at[0], near_cols.at[1], (az, rad_down, ax)),
    ]
    for copy in halos:
        copy.start()

    def grid(first, rows, columns):
        a = iota((rows, columns), 0).astype(F32)
        b = iota((rows, columns), 1).astype(F32)
        return cos_sin(wrapped(first * a * b))

    fine[0], fine[1] = grid(1.0, 16, CYCLE)
    coarse[0], coarse[1] = grid(16.0, MODES // 16, CYCLE)

    def forward_rows(i, carry):
        c0, s0 = fine[0], fine[1]
        c1, s1 = coarse[0, pl.ds(i, 1), :], coarse[1, pl.ds(i, 1), :]
        forward[pl.ds(pl.multiple_of(i * 16, 16), 16), :] = (c1 * c0 - s1 * s0).astype(BF16)
        forward[pl.ds(pl.multiple_of(MODES + i * 16, 16), 16), :] = (s1 * c0 + c1 * s0).astype(BF16)
        return carry

    lax.fori_loop(0, MODES // 16, forward_rows, 0)

    weight_k = jnp.where(iota((16, MODES), 1) == 0, 1.0, 2.0).astype(F32) / CYCLE
    fine[0, :, :MODES] = fine[0, :, :MODES] * weight_k
    fine[1, :, :MODES] = fine[1, :, :MODES] * weight_k
    c, s = grid(16.0, CYCLE // 16, MODES)
    for n in range(3):
        coarse[0, :, n * MODES : (n + 1) * MODES] = c[n * 32 : (n + 1) * 32]
        coarse[1, :, n * MODES : (n + 1) * MODES] = s[n * 32 : (n + 1) * 32]
    for n in range(3):

        def back_rows(i, carry, n=n):
            c0, s0 = fine[0, :, :MODES], fine[1, :, :MODES]
            c1 = coarse[0, pl.ds(i, 1), n * MODES : (n + 1) * MODES]
            s1 = coarse[1, pl.ds(i, 1), n * MODES : (n + 1) * MODES]
            rows = pl.ds(pl.multiple_of((n * 32 + i) * 16, 16), 16)
            back[rows, :MODES] = (c1 * c0 - s1 * s0).astype(BF16)
            back[rows, MODES:] = (s1 * c0 + c1 * s0).astype(BF16)
            return carry

        lax.fori_loop(0, 32, back_rows, 0)

    shift = ((2 * ax - 1) * rotor_step[0]).astype(F32)
    phase[0], phase[1] = cos_sin(wrapped(iota((MODES, LANES), 0).astype(F32) * shift))

    def transform(part):
        pltpu.make_async_copy(cycles.at[part], cycles.at[part], recv1.at[part]).wait()
        step = MODES // 2

        def ahead(i, carry):
            rows = pl.ds(pl.multiple_of(i * step, step), step)
            sine_rows = pl.ds(pl.multiple_of(MODES + i * step, step), step)
            cells = cycles[part].reshape(CYCLE, LANES)
            c = jnp.dot(forward[rows, :], cells, preferred_element_type=F32)
            d = jnp.dot(forward[sine_rows, :], cells, preferred_element_type=F32)
            cos_p, sin_p = phase[0, rows, :], phase[1, rows, :]
            spun[rows, :] = (c * cos_p - d * sin_p).astype(BF16)
            spun[sine_rows, :] = (c * sin_p + d * cos_p).astype(BF16)
            return carry

        lax.fori_loop(0, 2, ahead, 0)

        def astern(i, carry):
            rows = pl.ds(pl.multiple_of(i * (CYCLE // 4), CYCLE // 4), CYCLE // 4)
            cells = jnp.dot(back[rows, :], spun[...], preferred_element_type=F32).astype(BF16)
            rebuilt[part, pl.ds(i * COLS, COLS)] = cells.reshape(COLS, CELLS, LANES)
            return carry

        lax.fori_loop(0, 4, astern, 0)
        pltpu.make_async_copy(rebuilt.at[part, az], carried.at[part, az], recv2.at[part]).start()

        def send(k, carry):
            j = partner(k)
            pltpu.make_async_remote_copy(
                src_ref=rebuilt.at[part, j],
                dst_ref=carried.at[part, az],
                send_sem=send2.at[part],
                recv_sem=recv2.at[part],
                device_id=(j, rad, ax),
                device_id_type=MESH,
            ).start()
            return carry

        lax.fori_loop(1, RING, send, 0)

    lane = iota((GROUP, CELLS, LANES), 2)
    cell = iota((GROUP, CELLS, LANES), 1)

    def around(ref, i, slot, last):
        here = ref[pl.ds(i * GROUP, GROUP)].astype(F32)
        below = ref[pl.ds(jnp.maximum(i * GROUP - 1, 0), 1)].astype(F32)
        above = ref[pl.ds(jnp.minimum(i * GROUP + GROUP, last), 1)].astype(F32)
        plane_down = jnp.concatenate([below, here[:-1]], axis=0)
        plane_up = jnp.concatenate([here[1:], above], axis=0)
        rows = pl.ds(pl.multiple_of(slot * GROUP, GROUP), GROUP)
        cell_down = jnp.where(cell == 0, near_rows32[0, rows, :][:, None, :], pltpu.roll(here, 1, 1))
        cell_up = jnp.where(cell == CELLS - 1, near_rows32[1, rows, :][:, None, :], pltpu.roll(here, CELLS - 1, 1))
        half = lax.rem(slot, 2) * (GROUP * CELLS)
        columns = near_cols_t[pl.ds(pl.multiple_of(half, GROUP * CELLS), GROUP * CELLS), :].astype(BF16)
        pair = slot // 2
        r, l = iota((32, LANES), 0), iota((32, LANES), 1)
        place = ((r == pair) & (l == 0)) | ((r == pair + 16) & (l == LANES - 1))
        beyond = jnp.dot(columns, jnp.where(place, 1.0, 0.0).astype(BF16), preferred_element_type=F32)
        beyond = beyond.reshape(GROUP, CELLS, LANES)
        radius_down = jnp.where(lane == 0, beyond, pltpu.roll(here, 1, 2))
        radius_up = jnp.where(lane == LANES - 1, beyond, pltpu.roll(here, LANES - 1, 2))
        return here, plane_down, plane_up, cell_down, cell_up, radius_down, radius_up

    def side_weight(plane):
        middle = (plane.astype(F32) + 0.5) / PLANES
        return jnp.where(ax == 0, middle, 1.0 - middle)

    def faces(i, carry):
        here, plane_down, plane_up, *others = around(diffusivity, i, ROWS // GROUP + i, PLANES - 1)
        plane = iota((GROUP, CELLS, LANES), 0) + i * GROUP
        planes = pl.ds(i * GROUP, GROUP)
        first, final = plane == 0, plane == PLANES - 1
        down = 0.5 * (here + jnp.where(first, 0.0, plane_down))
        up = 0.5 * (here + jnp.where(final, 0.0, plane_up))
        total = down + up
        face_x[0, planes] = jnp.where(first, 0.0, down)
        face_x[1, planes] = jnp.where(final, 0.0, up)
        for n, other in enumerate(others):
            between = 0.5 * (here + other)
            face[n, planes] = between
            total = total + between
        face[4, planes] = 1.0 - total - side_weight(plane)
        return carry

    def flux(i, carry):
        here, plane_down, plane_up, *others = around(state, i, i, ROWS - 1)
        planes = pl.ds(lax.rem(i, PLANES // GROUP) * GROUP, GROUP)
        total = face[4, planes] * here
        total = total + face_x[0, planes] * plane_down
        total = total + face_x[1, planes] * plane_up
        for n, other in enumerate(others):
            total = total + face[n, planes] * other
        base[pl.ds(i * GROUP, GROUP)] = total
        return carry

    def blend(part):
        pltpu.make_async_copy(carried.at[part], carried.at[part], recv2.at[part]).wait()

        def some(i, carry):
            weight = side_weight(lax.rem(i, PLANES // GROUP) * GROUP + iota((GROUP, CELLS, LANES), 0))
            rows = pl.ds(part * RING + i * GROUP, GROUP)
            out[rows] = (base[rows] + weight * carried[part, pl.ds(i * GROUP, GROUP)].astype(F32)).astype(BF16)
            return carry

        lax.fori_loop(0, RING // GROUP, some, 0)

    transform(0)

    for copy in halos:
        copy.wait()

    def widen(i, carry):
        rows = pl.ds(pl.multiple_of(i * 16, 16), 16)
        near_rows32[0, rows, :] = near_rows[0, rows, :].astype(F32)
        near_rows32[1, rows, :] = near_rows[1, rows, :].astype(F32)
        return carry

    lax.fori_loop(0, (ROWS + PLANES) // 16, widen, 0)
    low = jnp.where(rad == 0, 0.0, near_cols[0].astype(F32))
    high = jnp.where(rad == 3, 0.0, near_cols[1].astype(F32))
    near_cols_t[...] = jnp.concatenate([low, high], axis=0).T
    lax.fori_loop(0, PLANES // GROUP, faces, 0)
    lax.fori_loop(0, ROWS // GROUP, flux, 0)

    for part in range(1, PARTS):
        transform(part)
    for part in range(PARTS):
        blend(part)
    for part in range(PARTS):
        pltpu.make_async_copy(cycles.at[part], cycles.at[part], send1.at[part]).wait()
        sent = rebuilt.at[part, pl.ds(0, RING - 1)]
        pltpu.make_async_copy(sent, sent, send2.at[part]).wait()


def body(state, diffusivity, rotor_step):
    vmem = pl.BlockSpec(memory_space=pltpu.VMEM)
    block = (PARTS, RING, CELLS, LANES)
    result = pl.pallas_call(
        kernel,
        out_shape=jax.ShapeDtypeStruct((ROWS, CELLS, LANES), BF16),
        in_specs=[vmem, vmem, pl.BlockSpec(memory_space=pltpu.SMEM)],
        out_specs=vmem,
        scratch_shapes=[
            pltpu.VMEM(block, BF16),
            pltpu.VMEM(block, BF16),
            pltpu.VMEM(block, BF16),
            pltpu.VMEM((ROWS, CELLS, LANES), F32),
            pltpu.VMEM((2 * MODES, CYCLE), BF16),
            pltpu.VMEM((CYCLE, 2 * MODES), BF16),
            pltpu.VMEM((2 * MODES, LANES), BF16),
            pltpu.VMEM((2, MODES, LANES), F32),
            pltpu.VMEM((2, 16, CYCLE), F32),
            pltpu.VMEM((2, MODES // 16, CYCLE), F32),
            pltpu.VMEM((2, ROWS + PLANES, LANES), BF16),
            pltpu.VMEM((2, ROWS + PLANES, LANES), BF16),
            pltpu.VMEM((2, ROWS + PLANES, LANES), F32),
            pltpu.VMEM((2, 16, 16 * CELLS), BF16),
            pltpu.VMEM((2, 16, 16 * CELLS), BF16),
            pltpu.VMEM((16 * CELLS, 32), F32),
            pltpu.VMEM((2, PLANES, CELLS, LANES), F32),
            pltpu.VMEM((5, PLANES, CELLS, LANES), F32),
            pltpu.SemaphoreType.DMA((PARTS,)),
            pltpu.SemaphoreType.DMA((PARTS,)),
            pltpu.SemaphoreType.DMA((PARTS,)),
            pltpu.SemaphoreType.DMA((PARTS,)),
            pltpu.SemaphoreType.DMA((4,)),
            pltpu.SemaphoreType.DMA((4,)),
        ],
        compiler_params=pltpu.CompilerParams(
            collective_id=0, has_side_effects=True, vmem_limit_bytes=48 * 1024 * 1024
        ),
    )(state.reshape(ROWS, CELLS, LANES), diffusivity.reshape(PLANES, CELLS, LANES), rotor_step)
    return result.reshape(1, FIELDS, PLANES, CELLS, LANES)


def solution(mesh):
    return jax.shard_map(
        body,
        mesh=mesh,
        in_specs=(P("ax", None, None, "az", "rad"), P("ax", None, "az", "rad"), P()),
        out_specs=P("ax", None, None, "az", "rad"),
        check_vma=False,
    )
```

```python
import functools
import math

import jax
import jax.numpy as jnp
from jax import lax
from jax.experimental import pallas as pl
from jax.experimental.pallas import tpu as pltpu
from jax.sharding import PartitionSpec as P

CYCLE = 1536
MODES = 512
FIELDS = 6
PLANES = 32
ROWS = FIELDS * PLANES
CELLS = 24
LANES = 128
RING = 64
COLS = 16
FAR = COLS // 2
NEAR = 5
PARTS = 3
GROUP = 8
MESH = pl.DeviceIdType.MESH
F32 = jnp.float32
BF16 = jnp.bfloat16


def iota(shape, dim):
    return lax.broadcasted_iota(jnp.int32, shape, dim)


def wrapped(product):
    left = product - jnp.floor(product * (1.0 / CYCLE)) * float(CYCLE)
    left = jnp.where(left < 0.0, left + float(CYCLE), left)
    return jnp.where(left >= float(CYCLE), left - float(CYCLE), left)


def cos_sin(cells):
    quarter = jnp.floor(cells * (4.0 / CYCLE) + 0.5)
    t = (cells - quarter * (CYCLE / 4.0)) * (2.0 * math.pi / CYCLE)
    u = t * t
    sine = t * (1.0 + u * (-1.0 / 6 + u * (1.0 / 120 + u * (-1.0 / 5040 + u * (1.0 / 362880)))))
    cosine = 1.0 + u * (-0.5 + u * (1.0 / 24 + u * (-1.0 / 720 + u * (1.0 / 40320 - u * (1.0 / 3628800)))))
    odd = (quarter == 1.0) | (quarter == 3.0)
    c = jnp.where(odd, sine, cosine)
    s = jnp.where(odd, cosine, sine)
    c = jnp.where((quarter == 1.0) | (quarter == 2.0), -c, c)
    s = jnp.where((quarter == 2.0) | (quarter == 3.0), -s, s)
    return c, s


def kernel(
    state_hbm,
    diffusivity_hbm,
    rotor_step,
    out,
    cycles,
    rebuilt,
    carried,
    base,
    forward,
    back,
    spun,
    phase,
    fine,
    coarse,
    edge_rows,
    near_rows,
    near_rows32,
    edge_cols,
    near_cols,
    near_cols_t,
    face_x,
    face,
    send1,
    recv1,
    send2,
    recv2,
    send_h,
    recv_h,
    state,
    diffusivity,
    load,
    known_below,
    known_above,
):
    az, rad, ax = lax.axis_index("az"), lax.axis_index("rad"), lax.axis_index("ax")
    x, z = az // COLS, lax.rem(az, COLS)
    az_up, az_down = lax.rem(az + 1, RING), lax.rem(az + RING - 1, RING)
    rad_up, rad_down = lax.rem(rad + 1, 4), lax.rem(rad + 3, 4)

    z_up, z_down = lax.rem(z + 1, COLS), lax.rem(z + COLS - 1, COLS)
    loads = [
        pltpu.make_async_copy(state_hbm, state, load.at[0]),
        pltpu.make_async_copy(diffusivity_hbm, diffusivity, load.at[1]),
    ]
    for copy in loads:
        copy.start()

    def signal(semaphore, *device):
        pl.semaphore_signal(semaphore, inc=1, device_id=device, device_id_type=MESH)

    barrier = pltpu.get_barrier_semaphore()
    for turn in range(4):
        run = lax.rem(x + turn, 4) * COLS
        for side in (ax, 1 - ax):
            signal(barrier, run + z_up, rad, side)
            signal(barrier, run + z_down, rad, side)
        signal(barrier, run + z, rad, 1 - ax)
        if turn:
            signal(barrier, run + z, rad, ax)
    signal(barrier, az, rad_up, ax)
    signal(barrier, az, rad_down, ax)
    pl.semaphore_wait(barrier, 25)
    signal(known_below.at[2], x * COLS + z_up, rad, ax)
    signal(known_above.at[2], x * COLS + z_down, rad, ax)
    for copy in loads:
        copy.wait()

    def place(turn, dz):
        return lax.rem(x + turn, 4) * COLS + lax.rem(z + dz, COLS)

    def send_plane(first, count, dz):
        def send(k, carry):
            part, j = first + k // 4, place(lax.rem(k, 4), dz)
            pltpu.make_async_remote_copy(
                src_ref=state.at[part * RING + j],
                dst_ref=cycles.at[part, az],
                send_sem=send1.at[part],
                recv_sem=recv1.at[part],
                device_id=(j, rad, 1 - ax),
                device_id_type=MESH,
            ).start()
            return carry

        lax.fori_loop(0, 4 * count, send, 0)

    def send_both(first, count, far):
        send_plane(first, count, far)
        send_plane(first, count, COLS - far)

    send_plane(0, PARTS, 0)
    send_both(0, PARTS, 1)

    def reach(far, carry, count):
        pl.semaphore_wait(known_below.at[far], 1)
        signal(known_below.at[far + 1], x * COLS + z_up, rad, ax)
        pl.semaphore_wait(known_above.at[far], 1)

        @pl.when(far < FAR - 1)
        def _():
            signal(known_above.at[far + 1], x * COLS + z_down, rad, ax)

        send_both(0, count, far)
        return carry

    lax.fori_loop(2, NEAR + 1, functools.partial(reach, count=PARTS), 0)
    lax.fori_loop(NEAR + 1, FAR, functools.partial(reach, count=1), 0)
    pl.semaphore_wait(known_below.at[FAR], 1)
    send_plane(0, PARTS, FAR)

    def send_rest(i, carry):
        send_both(1 + i // (FAR - 1 - NEAR), 1, FAR - 1 - lax.rem(i, FAR - 1 - NEAR))
        return carry

    lax.fori_loop(0, (PARTS - 1) * (FAR - 1 - NEAR), send_rest, 0)

    def edges(ref, i, slot, acc):
        block = ref[pl.ds(pl.multiple_of(i * 16, 16), 16)]
        wide = block.astype(F32)
        rows = pl.ds(pl.multiple_of(slot * 16, 16), 16)
        edge_rows[0, rows, :] = wide[:, 0, :].astype(BF16)
        edge_rows[1, rows, :] = wide[:, CELLS - 1, :].astype(BF16)
        row, lane = iota((32, LANES), 0), iota((32, LANES), 1)
        pick = ((row == slot) & (lane == 0)) | ((row == slot + 16) & (lane == LANES - 1))
        return acc + lax.dot_general(
            jnp.where(pick, 1.0, 0.0).astype(BF16),
            block.reshape(16 * CELLS, LANES),
            (((1,), (1,)), ((), ())),
            preferred_element_type=F32,
        )

    acc = jnp.zeros((32, 16 * CELLS), F32)
    acc = lax.fori_loop(0, ROWS // 16, lambda i, a: edges(state, i, i, a), acc)
    acc = lax.fori_loop(0, PLANES // 16, lambda i, a: edges(diffusivity, i, i + ROWS // 16, a), acc)
    edge_cols[0] = acc[:16].astype(BF16)
    edge_cols[1] = acc[16:].astype(BF16)

    def halo(n, src, dst, target):
        return pltpu.make_async_remote_copy(
            src_ref=src, dst_ref=dst, send_sem=send_h.at[n], recv_sem=recv_h.at[n],
            device_id=target, device_id_type=MESH,
        )

    halos = [
        halo(0, edge_rows.at[1], near_rows.at[0], (az_up, rad, ax)),
        halo(1, edge_rows.at[0], near_rows.at[1], (az_down, rad, ax)),
        halo(2, edge_cols.at[1], near_cols.at[0], (az, rad_up, ax)),
        halo(3, edge_cols.at[0], near_cols.at[1], (az, rad_down, ax)),
    ]
    for copy in halos:
        copy.start()

    def grid(first, rows, columns):
        a = iota((rows, columns), 0).astype(F32)
        b = iota((rows, columns), 1).astype(F32)
        return cos_sin(wrapped(first * a * b))

    fine[0], fine[1] = grid(1.0, 16, CYCLE)
    coarse[0], coarse[1] = grid(16.0, MODES // 16, CYCLE)

    def forward_rows(i, carry):
        c0, s0 = fine[0], fine[1]
        c1, s1 = coarse[0, pl.ds(i, 1), :], coarse[1, pl.ds(i, 1), :]
        forward[pl.ds(pl.multiple_of(i * 16, 16), 16), :] = (c1 * c0 - s1 * s0).astype(BF16)
        forward[pl.ds(pl.multiple_of(MODES + i * 16, 16), 16), :] = (s1 * c0 + c1 * s0).astype(BF16)
        return carry

    lax.fori_loop(0, MODES // 16, forward_rows, 0)

    weight_k = jnp.where(iota((16, MODES), 1) == 0, 1.0, 2.0).astype(F32) / CYCLE
    fine[0, :, :MODES] = fine[0, :, :MODES] * weight_k
    fine[1, :, :MODES] = fine[1, :, :MODES] * weight_k
    c, s = grid(16.0, CYCLE // 16, MODES)
    for n in range(3):
        coarse[0, :, n * MODES : (n + 1) * MODES] = c[n * 32 : (n + 1) * 32]
        coarse[1, :, n * MODES : (n + 1) * MODES] = s[n * 32 : (n + 1) * 32]
    for n in range(3):

        def back_rows(i, carry, n=n):
            c0, s0 = fine[0, :, :MODES], fine[1, :, :MODES]
            c1 = coarse[0, pl.ds(i, 1), n * MODES : (n + 1) * MODES]
            s1 = coarse[1, pl.ds(i, 1), n * MODES : (n + 1) * MODES]
            rows = pl.ds(pl.multiple_of((n * 32 + i) * 16, 16), 16)
            back[rows, :MODES] = (c1 * c0 - s1 * s0).astype(BF16)
            back[rows, MODES:] = (s1 * c0 + c1 * s0).astype(BF16)
            return carry

        lax.fori_loop(0, 32, back_rows, 0)

    shift = ((2 * ax - 1) * rotor_step[0]).astype(F32)
    phase[0], phase[1] = cos_sin(wrapped(iota((MODES, LANES), 0).astype(F32) * shift))

    def transform(part):
        pltpu.make_async_copy(cycles.at[part], cycles.at[part], recv1.at[part]).wait()
        step = MODES // 2

        def ahead(i, carry):
            rows = pl.ds(pl.multiple_of(i * step, step), step)
            sine_rows = pl.ds(pl.multiple_of(MODES + i * step, step), step)
            cells = cycles[part].reshape(CYCLE, LANES)
            c = jnp.dot(forward[rows, :], cells, preferred_element_type=F32)
            d = jnp.dot(forward[sine_rows, :], cells, preferred_element_type=F32)
            cos_p, sin_p = phase[0, rows, :], phase[1, rows, :]
            spun[rows, :] = (c * cos_p - d * sin_p).astype(BF16)
            spun[sine_rows, :] = (c * sin_p + d * cos_p).astype(BF16)
            return carry

        lax.fori_loop(0, 2, ahead, 0)

        def astern(i, carry):
            rows = pl.ds(pl.multiple_of(i * (CYCLE // 4), CYCLE // 4), CYCLE // 4)
            cells = jnp.dot(back[rows, :], spun[...], preferred_element_type=F32).astype(BF16)
            rebuilt[part, pl.ds(i * COLS, COLS)] = cells.reshape(COLS, CELLS, LANES)
            return carry

        lax.fori_loop(0, 4, astern, 0)
        pltpu.make_async_copy(rebuilt.at[part, az], carried.at[part, az], recv2.at[part]).start()

        def send(k, carry):
            m = COLS - 1 - k // 4
            far = (m + 1) // 2
            j = place(lax.rem(k, 4), jnp.where(lax.rem(m, 2) == 1, far, COLS - far))
            pltpu.make_async_remote_copy(
                src_ref=rebuilt.at[part, j],
                dst_ref=carried.at[part, az],
                send_sem=send2.at[part],
                recv_sem=recv2.at[part],
                device_id=(j, rad, ax),
                device_id_type=MESH,
            ).start()
            return carry

        lax.fori_loop(0, RING - 4, send, 0)
        lax.fori_loop(RING - 3, RING, send, 0)

    lane = iota((GROUP, CELLS, LANES), 2)
    cell = iota((GROUP, CELLS, LANES), 1)

    def around(ref, i, slot, last):
        here = ref[pl.ds(i * GROUP, GROUP)].astype(F32)
        below = ref[pl.ds(jnp.maximum(i * GROUP - 1, 0), 1)].astype(F32)
        above = ref[pl.ds(jnp.minimum(i * GROUP + GROUP, last), 1)].astype(F32)
        plane_down = jnp.concatenate([below, here[:-1]], axis=0)
        plane_up = jnp.concatenate([here[1:], above], axis=0)
        rows = pl.ds(pl.multiple_of(slot * GROUP, GROUP), GROUP)
        cell_down = jnp.where(cell == 0, near_rows32[0, rows, :][:, None, :], pltpu.roll(here, 1, 1))
        cell_up = jnp.where(cell == CELLS - 1, near_rows32[1, rows, :][:, None, :], pltpu.roll(here, CELLS - 1, 1))
        half = lax.rem(slot, 2) * (GROUP * CELLS)
        columns = near_cols_t[pl.ds(pl.multiple_of(half, GROUP * CELLS), GROUP * CELLS), :].astype(BF16)
        pair = slot // 2
        r, l = iota((32, LANES), 0), iota((32, LANES), 1)
        place = ((r == pair) & (l == 0)) | ((r == pair + 16) & (l == LANES - 1))
        beyond = jnp.dot(columns, jnp.where(place, 1.0, 0.0).astype(BF16), preferred_element_type=F32)
        beyond = beyond.reshape(GROUP, CELLS, LANES)
        radius_down = jnp.where(lane == 0, beyond, pltpu.roll(here, 1, 2))
        radius_up = jnp.where(lane == LANES - 1, beyond, pltpu.roll(here, LANES - 1, 2))
        return here, plane_down, plane_up, cell_down, cell_up, radius_down, radius_up

    def side_weight(plane):
        middle = (plane.astype(F32) + 0.5) / PLANES
        return jnp.where(ax == 0, middle, 1.0 - middle)

    def faces(i, carry):
        here, plane_down, plane_up, *others = around(diffusivity, i, ROWS // GROUP + i, PLANES - 1)
        plane = iota((GROUP, CELLS, LANES), 0) + i * GROUP
        planes = pl.ds(i * GROUP, GROUP)
        first, final = plane == 0, plane == PLANES - 1
        down = 0.5 * (here + jnp.where(first, 0.0, plane_down))
        up = 0.5 * (here + jnp.where(final, 0.0, plane_up))
        total = down + up
        face_x[0, planes] = jnp.where(first, 0.0, down)
        face_x[1, planes] = jnp.where(final, 0.0, up)
        for n, other in enumerate(others):
            between = 0.5 * (here + other)
            face[n, planes] = between
            total = total + between
        face[4, planes] = 1.0 - total - side_weight(plane)
        return carry

    def flux(i, carry):
        here, plane_down, plane_up, *others = around(state, i, i, ROWS - 1)
        planes = pl.ds(lax.rem(i, PLANES // GROUP) * GROUP, GROUP)
        total = face[4, planes] * here
        total = total + face_x[0, planes] * plane_down
        total = total + face_x[1, planes] * plane_up
        for n, other in enumerate(others):
            total = total + face[n, planes] * other
        base[pl.ds(i * GROUP, GROUP)] = total
        return carry

    def blend(part):
        pltpu.make_async_copy(carried.at[part], carried.at[part], recv2.at[part]).wait()

        def some(i, carry):
            weight = side_weight(lax.rem(i, PLANES // GROUP) * GROUP + iota((GROUP, CELLS, LANES), 0))
            rows = pl.ds(part * RING + i * GROUP, GROUP)
            out[rows] = (base[rows] + weight * carried[part, pl.ds(i * GROUP, GROUP)].astype(F32)).astype(BF16)
            return carry

        lax.fori_loop(0, RING // GROUP, some, 0)

    transform(0)

    for copy in halos:
        copy.wait()

    def widen(i, carry):
        rows = pl.ds(pl.multiple_of(i * 16, 16), 16)
        near_rows32[0, rows, :] = near_rows[0, rows, :].astype(F32)
        near_rows32[1, rows, :] = near_rows[1, rows, :].astype(F32)
        return carry

    lax.fori_loop(0, (ROWS + PLANES) // 16, widen, 0)
    low = jnp.where(rad == 0, 0.0, near_cols[0].astype(F32))
    high = jnp.where(rad == 3, 0.0, near_cols[1].astype(F32))
    near_cols_t[...] = jnp.concatenate([low, high], axis=0).T
    lax.fori_loop(0, PLANES // GROUP, faces, 0)
    lax.fori_loop(0, ROWS // GROUP, flux, 0)

    for part in range(1, PARTS):
        transform(part)
    for part in range(PARTS):
        blend(part)
    for part in range(PARTS):
        pltpu.make_async_copy(cycles.at[part], cycles.at[part], send1.at[part]).wait()
        sent = rebuilt.at[part, pl.ds(0, RING - 1)]
        pltpu.make_async_copy(sent, sent, send2.at[part]).wait()


def body(state, diffusivity, rotor_step):
    vmem = pl.BlockSpec(memory_space=pltpu.VMEM)
    hbm = pl.BlockSpec(memory_space=pltpu.HBM)
    block = (PARTS, RING, CELLS, LANES)
    result = pl.pallas_call(
        kernel,
        out_shape=jax.ShapeDtypeStruct((ROWS, CELLS, LANES), BF16),
        in_specs=[hbm, hbm, pl.BlockSpec(memory_space=pltpu.SMEM)],
        out_specs=vmem,
        scratch_shapes=[
            pltpu.VMEM(block, BF16),
            pltpu.VMEM(block, BF16),
            pltpu.VMEM(block, BF16),
            pltpu.VMEM((ROWS, CELLS, LANES), F32),
            pltpu.VMEM((2 * MODES, CYCLE), BF16),
            pltpu.VMEM((CYCLE, 2 * MODES), BF16),
            pltpu.VMEM((2 * MODES, LANES), BF16),
            pltpu.VMEM((2, MODES, LANES), F32),
            pltpu.VMEM((2, 16, CYCLE), F32),
            pltpu.VMEM((2, MODES // 16, CYCLE), F32),
            pltpu.VMEM((2, ROWS + PLANES, LANES), BF16),
            pltpu.VMEM((2, ROWS + PLANES, LANES), BF16),
            pltpu.VMEM((2, ROWS + PLANES, LANES), F32),
            pltpu.VMEM((2, 16, 16 * CELLS), BF16),
            pltpu.VMEM((2, 16, 16 * CELLS), BF16),
            pltpu.VMEM((16 * CELLS, 32), F32),
            pltpu.VMEM((2, PLANES, CELLS, LANES), F32),
            pltpu.VMEM((5, PLANES, CELLS, LANES), F32),
            pltpu.SemaphoreType.DMA((PARTS,)),
            pltpu.SemaphoreType.DMA((PARTS,)),
            pltpu.SemaphoreType.DMA((PARTS,)),
            pltpu.SemaphoreType.DMA((PARTS,)),
            pltpu.SemaphoreType.DMA((4,)),
            pltpu.SemaphoreType.DMA((4,)),
            pltpu.VMEM((ROWS, CELLS, LANES), BF16),
            pltpu.VMEM((PLANES, CELLS, LANES), BF16),
            pltpu.SemaphoreType.DMA((2,)),
            pltpu.SemaphoreType.REGULAR((FAR + 1,)),
            pltpu.SemaphoreType.REGULAR((FAR + 1,)),
        ],
        compiler_params=pltpu.CompilerParams(
            collective_id=0, has_side_effects=True, vmem_limit_bytes=52 * 1024 * 1024
        ),
    )(state.reshape(ROWS, CELLS, LANES), diffusivity.reshape(PLANES, CELLS, LANES), rotor_step)
    return result.reshape(1, FIELDS, PLANES, CELLS, LANES)


def solution(mesh):
    return jax.shard_map(
        body,
        mesh=mesh,
        in_specs=(P("ax", None, None, "az", "rad"), P("ax", None, "az", "rad"), P()),
        out_specs=P("ax", None, None, "az", "rad"),
        check_vma=False,
    )
```

```python
import functools
import math

import jax
import jax.numpy as jnp
from jax import lax
from jax.experimental import pallas as pl
from jax.experimental.pallas import tpu as pltpu
from jax.sharding import PartitionSpec as P

CYCLE = 1536
MODES = 512
FIELDS = 6
PLANES = 32
ROWS = FIELDS * PLANES
CELLS = 24
LANES = 128
RING = 64
COLS = 16
FAR = COLS // 2
NEAR = 4
PARTS = 3
GROUP = 8
MESH = pl.DeviceIdType.MESH
F32 = jnp.float32
BF16 = jnp.bfloat16


def iota(shape, dim):
    return lax.broadcasted_iota(jnp.int32, shape, dim)


def wrapped(product):
    left = product - jnp.floor(product * (1.0 / CYCLE)) * float(CYCLE)
    left = jnp.where(left < 0.0, left + float(CYCLE), left)
    return jnp.where(left >= float(CYCLE), left - float(CYCLE), left)


def cos_sin(cells):
    quarter = jnp.floor(cells * (4.0 / CYCLE) + 0.5)
    t = (cells - quarter * (CYCLE / 4.0)) * (2.0 * math.pi / CYCLE)
    u = t * t
    sine = t * (1.0 + u * (-1.0 / 6 + u * (1.0 / 120 + u * (-1.0 / 5040 + u * (1.0 / 362880)))))
    cosine = 1.0 + u * (-0.5 + u * (1.0 / 24 + u * (-1.0 / 720 + u * (1.0 / 40320 - u * (1.0 / 3628800)))))
    odd = (quarter == 1.0) | (quarter == 3.0)
    c = jnp.where(odd, sine, cosine)
    s = jnp.where(odd, cosine, sine)
    c = jnp.where((quarter == 1.0) | (quarter == 2.0), -c, c)
    s = jnp.where((quarter == 2.0) | (quarter == 3.0), -s, s)
    return c, s


def kernel(
    state_hbm,
    diffusivity_hbm,
    rotor_step,
    out,
    cycles,
    rebuilt,
    carried,
    base,
    forward,
    back,
    spun,
    phase,
    fine,
    coarse,
    edge_rows,
    near_rows,
    near_rows32,
    edge_cols,
    near_cols,
    near_cols_t,
    face_x,
    face,
    send1,
    recv1,
    send2,
    recv2,
    send_h,
    recv_h,
    state,
    diffusivity,
    load,
    known_below,
    known_above,
):
    az, rad, ax = lax.axis_index("az"), lax.axis_index("rad"), lax.axis_index("ax")
    x, z = az // COLS, lax.rem(az, COLS)
    az_up, az_down = lax.rem(az + 1, RING), lax.rem(az + RING - 1, RING)
    rad_up, rad_down = lax.rem(rad + 1, 4), lax.rem(rad + 3, 4)

    z_up, z_down = lax.rem(z + 1, COLS), lax.rem(z + COLS - 1, COLS)
    loads = [
        pltpu.make_async_copy(state_hbm, state, load.at[0]),
        pltpu.make_async_copy(diffusivity_hbm, diffusivity, load.at[1]),
    ]
    for copy in loads:
        copy.start()

    def signal(semaphore, *device):
        pl.semaphore_signal(semaphore, inc=1, device_id=device, device_id_type=MESH)

    barrier = pltpu.get_barrier_semaphore()
    for turn in range(4):
        run = lax.rem(x + turn, 4) * COLS
        for side in (ax, 1 - ax):
            signal(barrier, run + z_up, rad, side)
            signal(barrier, run + z_down, rad, side)
        signal(barrier, run + z, rad, 1 - ax)
        if turn:
            signal(barrier, run + z, rad, ax)
    signal(barrier, az, rad_up, ax)
    signal(barrier, az, rad_down, ax)
    pl.semaphore_wait(barrier, 25)
    signal(known_below.at[2], x * COLS + z_up, rad, ax)
    signal(known_above.at[2], x * COLS + z_down, rad, ax)
    for copy in loads:
        copy.wait()

    def place(turn, dz):
        return lax.rem(x + turn, 4) * COLS + lax.rem(z + dz, COLS)

    def send_plane(first, count, dz):
        def send(k, carry):
            part, j = first + k // 4, place(lax.rem(k, 4), dz)
            pltpu.make_async_remote_copy(
                src_ref=state.at[part * RING + j],
                dst_ref=cycles.at[part, az],
                send_sem=send1.at[part],
                recv_sem=recv1.at[part],
                device_id=(j, rad, 1 - ax),
                device_id_type=MESH,
            ).start()
            return carry

        lax.fori_loop(0, 4 * count, send, 0)

    def send_both(first, count, far):
        send_plane(first, count, far)
        send_plane(first, count, COLS - far)

    send_plane(0, PARTS, 0)
    send_both(0, PARTS, 1)

    def reach(far, carry, count):
        pl.semaphore_wait(known_below.at[far], 1)
        signal(known_below.at[far + 1], x * COLS + z_up, rad, ax)
        pl.semaphore_wait(known_above.at[far], 1)

        @pl.when(far < FAR - 1)
        def _():
            signal(known_above.at[far + 1], x * COLS + z_down, rad, ax)

        send_both(0, count, far)
        return carry

    lax.fori_loop(2, NEAR + 1, functools.partial(reach, count=PARTS), 0)
    lax.fori_loop(NEAR + 1, FAR, functools.partial(reach, count=1), 0)
    pl.semaphore_wait(known_below.at[FAR], 1)
    send_plane(0, PARTS, FAR)

    def send_rest(i, carry):
        send_both(1 + i // (FAR - 1 - NEAR), 1, FAR - 1 - lax.rem(i, FAR - 1 - NEAR))
        return carry

    lax.fori_loop(0, (PARTS - 1) * (FAR - 1 - NEAR), send_rest, 0)

    def edges(ref, i, slot, acc):
        block = ref[pl.ds(pl.multiple_of(i * 16, 16), 16)]
        wide = block.astype(F32)
        rows = pl.ds(pl.multiple_of(slot * 16, 16), 16)
        edge_rows[0, rows, :] = wide[:, 0, :].astype(BF16)
        edge_rows[1, rows, :] = wide[:, CELLS - 1, :].astype(BF16)
        row, lane = iota((32, LANES), 0), iota((32, LANES), 1)
        pick = ((row == slot) & (lane == 0)) | ((row == slot + 16) & (lane == LANES - 1))
        return acc + lax.dot_general(
            jnp.where(pick, 1.0, 0.0).astype(BF16),
            block.reshape(16 * CELLS, LANES),
            (((1,), (1,)), ((), ())),
            preferred_element_type=F32,
        )

    acc = jnp.zeros((32, 16 * CELLS), F32)
    acc = lax.fori_loop(0, ROWS // 16, lambda i, a: edges(state, i, i, a), acc)
    acc = lax.fori_loop(0, PLANES // 16, lambda i, a: edges(diffusivity, i, i + ROWS // 16, a), acc)
    edge_cols[0] = acc[:16].astype(BF16)
    edge_cols[1] = acc[16:].astype(BF16)

    def halo(n, src, dst, target):
        return pltpu.make_async_remote_copy(
            src_ref=src, dst_ref=dst, send_sem=send_h.at[n], recv_sem=recv_h.at[n],
            device_id=target, device_id_type=MESH,
        )

    halos = [
        halo(0, edge_rows.at[1], near_rows.at[0], (az_up, rad, ax)),
        halo(1, edge_rows.at[0], near_rows.at[1], (az_down, rad, ax)),
        halo(2, edge_cols.at[1], near_cols.at[0], (az, rad_up, ax)),
        halo(3, edge_cols.at[0], near_cols.at[1], (az, rad_down, ax)),
    ]
    for copy in halos:
        copy.start()

    def grid(first, rows, columns):
        a = iota((rows, columns), 0).astype(F32)
        b = iota((rows, columns), 1).astype(F32)
        return cos_sin(wrapped(first * a * b))

    fine[0], fine[1] = grid(1.0, 16, CYCLE)
    coarse[0], coarse[1] = grid(16.0, MODES // 16, CYCLE)

    def forward_rows(i, carry):
        c0, s0 = fine[0], fine[1]
        c1, s1 = coarse[0, pl.ds(i, 1), :], coarse[1, pl.ds(i, 1), :]
        forward[pl.ds(pl.multiple_of(i * 16, 16), 16), :] = (c1 * c0 - s1 * s0).astype(BF16)
        forward[pl.ds(pl.multiple_of(MODES + i * 16, 16), 16), :] = (s1 * c0 + c1 * s0).astype(BF16)
        return carry

    lax.fori_loop(0, MODES // 16, forward_rows, 0)

    weight_k = jnp.where(iota((16, MODES), 1) == 0, 1.0, 2.0).astype(F32) / CYCLE
    fine[0, :, :MODES] = fine[0, :, :MODES] * weight_k
    fine[1, :, :MODES] = fine[1, :, :MODES] * weight_k
    c, s = grid(16.0, CYCLE // 16, MODES)
    for n in range(3):
        coarse[0, :, n * MODES : (n + 1) * MODES] = c[n * 32 : (n + 1) * 32]
        coarse[1, :, n * MODES : (n + 1) * MODES] = s[n * 32 : (n + 1) * 32]
    for n in range(3):

        def back_rows(i, carry, n=n):
            c0, s0 = fine[0, :, :MODES], fine[1, :, :MODES]
            c1 = coarse[0, pl.ds(i, 1), n * MODES : (n + 1) * MODES]
            s1 = coarse[1, pl.ds(i, 1), n * MODES : (n + 1) * MODES]
            rows = pl.ds(pl.multiple_of((n * 32 + i) * 16, 16), 16)
            back[rows, :MODES] = (c1 * c0 - s1 * s0).astype(BF16)
            back[rows, MODES:] = (s1 * c0 + c1 * s0).astype(BF16)
            return carry

        lax.fori_loop(0, 32, back_rows, 0)

    shift = ((2 * ax - 1) * rotor_step[0]).astype(F32)
    phase[0], phase[1] = cos_sin(wrapped(iota((MODES, LANES), 0).astype(F32) * shift))

    def transform(part):
        pltpu.make_async_copy(cycles.at[part], cycles.at[part], recv1.at[part]).wait()
        step = MODES // 2

        def ahead(i, carry):
            rows = pl.ds(pl.multiple_of(i * step, step), step)
            sine_rows = pl.ds(pl.multiple_of(MODES + i * step, step), step)
            cells = cycles[part].reshape(CYCLE, LANES)
            c = jnp.dot(forward[rows, :], cells, preferred_element_type=F32)
            d = jnp.dot(forward[sine_rows, :], cells, preferred_element_type=F32)
            cos_p, sin_p = phase[0, rows, :], phase[1, rows, :]
            spun[rows, :] = (c * cos_p - d * sin_p).astype(BF16)
            spun[sine_rows, :] = (c * sin_p + d * cos_p).astype(BF16)
            return carry

        lax.fori_loop(0, 2, ahead, 0)

        def astern(i, carry):
            rows = pl.ds(pl.multiple_of(i * (CYCLE // 4), CYCLE // 4), CYCLE // 4)
            cells = jnp.dot(back[rows, :], spun[...], preferred_element_type=F32).astype(BF16)
            rebuilt[part, pl.ds(i * COLS, COLS)] = cells.reshape(COLS, CELLS, LANES)
            return carry

        lax.fori_loop(0, 4, astern, 0)
        pltpu.make_async_copy(rebuilt.at[part, az], carried.at[part, az], recv2.at[part]).start()

        def send(k, carry):
            m = COLS - 1 - k // 4
            far = (m + 1) // 2
            j = place(lax.rem(k, 4), jnp.where(lax.rem(m, 2) == 1, far, COLS - far))
            pltpu.make_async_remote_copy(
                src_ref=rebuilt.at[part, j],
                dst_ref=carried.at[part, az],
                send_sem=send2.at[part],
                recv_sem=recv2.at[part],
                device_id=(j, rad, ax),
                device_id_type=MESH,
            ).start()
            return carry

        lax.fori_loop(0, RING - 4, send, 0)
        lax.fori_loop(RING - 3, RING, send, 0)

    lane = iota((GROUP, CELLS, LANES), 2)
    cell = iota((GROUP, CELLS, LANES), 1)

    def around(ref, i, slot, last):
        here = ref[pl.ds(i * GROUP, GROUP)].astype(F32)
        below = ref[pl.ds(jnp.maximum(i * GROUP - 1, 0), 1)].astype(F32)
        above = ref[pl.ds(jnp.minimum(i * GROUP + GROUP, last), 1)].astype(F32)
        plane_down = jnp.concatenate([below, here[:-1]], axis=0)
        plane_up = jnp.concatenate([here[1:], above], axis=0)
        rows = pl.ds(pl.multiple_of(slot * GROUP, GROUP), GROUP)
        cell_down = jnp.where(cell == 0, near_rows32[0, rows, :][:, None, :], pltpu.roll(here, 1, 1))
        cell_up = jnp.where(cell == CELLS - 1, near_rows32[1, rows, :][:, None, :], pltpu.roll(here, CELLS - 1, 1))
        half = lax.rem(slot, 2) * (GROUP * CELLS)
        columns = near_cols_t[pl.ds(pl.multiple_of(half, GROUP * CELLS), GROUP * CELLS), :].astype(BF16)
        pair = slot // 2
        r, l = iota((32, LANES), 0), iota((32, LANES), 1)
        place = ((r == pair) & (l == 0)) | ((r == pair + 16) & (l == LANES - 1))
        beyond = jnp.dot(columns, jnp.where(place, 1.0, 0.0).astype(BF16), preferred_element_type=F32)
        beyond = beyond.reshape(GROUP, CELLS, LANES)
        radius_down = jnp.where(lane == 0, beyond, pltpu.roll(here, 1, 2))
        radius_up = jnp.where(lane == LANES - 1, beyond, pltpu.roll(here, LANES - 1, 2))
        return here, plane_down, plane_up, cell_down, cell_up, radius_down, radius_up

    def side_weight(plane):
        middle = (plane.astype(F32) + 0.5) / PLANES
        return jnp.where(ax == 0, middle, 1.0 - middle)

    def faces(i, carry):
        here, plane_down, plane_up, *others = around(diffusivity, i, ROWS // GROUP + i, PLANES - 1)
        plane = iota((GROUP, CELLS, LANES), 0) + i * GROUP
        planes = pl.ds(i * GROUP, GROUP)
        first, final = plane == 0, plane == PLANES - 1
        down = 0.5 * (here + jnp.where(first, 0.0, plane_down))
        up = 0.5 * (here + jnp.where(final, 0.0, plane_up))
        total = down + up
        face_x[0, planes] = jnp.where(first, 0.0, down)
        face_x[1, planes] = jnp.where(final, 0.0, up)
        for n, other in enumerate(others):
            between = 0.5 * (here + other)
            face[n, planes] = between
            total = total + between
        face[4, planes] = 1.0 - total - side_weight(plane)
        return carry

    def flux(i, carry):
        here, plane_down, plane_up, *others = around(state, i, i, ROWS - 1)
        planes = pl.ds(lax.rem(i, PLANES // GROUP) * GROUP, GROUP)
        total = face[4, planes] * here
        total = total + face_x[0, planes] * plane_down
        total = total + face_x[1, planes] * plane_up
        for n, other in enumerate(others):
            total = total + face[n, planes] * other
        base[pl.ds(i * GROUP, GROUP)] = total
        return carry

    def blend(part):
        pltpu.make_async_copy(carried.at[part], carried.at[part], recv2.at[part]).wait()

        def some(i, carry):
            weight = side_weight(lax.rem(i, PLANES // GROUP) * GROUP + iota((GROUP, CELLS, LANES), 0))
            rows = pl.ds(part * RING + i * GROUP, GROUP)
            out[rows] = (base[rows] + weight * carried[part, pl.ds(i * GROUP, GROUP)].astype(F32)).astype(BF16)
            return carry

        lax.fori_loop(0, RING // GROUP, some, 0)

    transform(0)

    for copy in halos:
        copy.wait()

    def widen(i, carry):
        rows = pl.ds(pl.multiple_of(i * 16, 16), 16)
        near_rows32[0, rows, :] = near_rows[0, rows, :].astype(F32)
        near_rows32[1, rows, :] = near_rows[1, rows, :].astype(F32)
        return carry

    lax.fori_loop(0, (ROWS + PLANES) // 16, widen, 0)
    low = jnp.where(rad == 0, 0.0, near_cols[0].astype(F32))
    high = jnp.where(rad == 3, 0.0, near_cols[1].astype(F32))
    near_cols_t[...] = jnp.concatenate([low, high], axis=0).T
    lax.fori_loop(0, PLANES // GROUP, faces, 0)
    lax.fori_loop(0, ROWS // GROUP, flux, 0)

    for part in range(1, PARTS):
        transform(part)
    for part in range(PARTS):
        blend(part)
    for part in range(PARTS):
        pltpu.make_async_copy(cycles.at[part], cycles.at[part], send1.at[part]).wait()
        sent = rebuilt.at[part, pl.ds(0, RING - 1)]
        pltpu.make_async_copy(sent, sent, send2.at[part]).wait()


def body(state, diffusivity, rotor_step):
    vmem = pl.BlockSpec(memory_space=pltpu.VMEM)
    hbm = pl.BlockSpec(memory_space=pltpu.HBM)
    block = (PARTS, RING, CELLS, LANES)
    result = pl.pallas_call(
        kernel,
        out_shape=jax.ShapeDtypeStruct((ROWS, CELLS, LANES), BF16),
        in_specs=[hbm, hbm, pl.BlockSpec(memory_space=pltpu.SMEM)],
        out_specs=vmem,
        scratch_shapes=[
            pltpu.VMEM(block, BF16),
            pltpu.VMEM(block, BF16),
            pltpu.VMEM(block, BF16),
            pltpu.VMEM((ROWS, CELLS, LANES), F32),
            pltpu.VMEM((2 * MODES, CYCLE), BF16),
            pltpu.VMEM((CYCLE, 2 * MODES), BF16),
            pltpu.VMEM((2 * MODES, LANES), BF16),
            pltpu.VMEM((2, MODES, LANES), F32),
            pltpu.VMEM((2, 16, CYCLE), F32),
            pltpu.VMEM((2, MODES // 16, CYCLE), F32),
            pltpu.VMEM((2, ROWS + PLANES, LANES), BF16),
            pltpu.VMEM((2, ROWS + PLANES, LANES), BF16),
            pltpu.VMEM((2, ROWS + PLANES, LANES), F32),
            pltpu.VMEM((2, 16, 16 * CELLS), BF16),
            pltpu.VMEM((2, 16, 16 * CELLS), BF16),
            pltpu.VMEM((16 * CELLS, 32), F32),
            pltpu.VMEM((2, PLANES, CELLS, LANES), F32),
            pltpu.VMEM((5, PLANES, CELLS, LANES), F32),
            pltpu.SemaphoreType.DMA((PARTS,)),
            pltpu.SemaphoreType.DMA((PARTS,)),
            pltpu.SemaphoreType.DMA((PARTS,)),
            pltpu.SemaphoreType.DMA((PARTS,)),
            pltpu.SemaphoreType.DMA((4,)),
            pltpu.SemaphoreType.DMA((4,)),
            pltpu.VMEM((ROWS, CELLS, LANES), BF16),
            pltpu.VMEM((PLANES, CELLS, LANES), BF16),
            pltpu.SemaphoreType.DMA((2,)),
            pltpu.SemaphoreType.REGULAR((FAR + 1,)),
            pltpu.SemaphoreType.REGULAR((FAR + 1,)),
        ],
        compiler_params=pltpu.CompilerParams(
            collective_id=0, has_side_effects=True, vmem_limit_bytes=52 * 1024 * 1024
        ),
    )(
        pltpu.with_memory_space_constraint(state.reshape(ROWS, CELLS, LANES), pltpu.HBM),
        pltpu.with_memory_space_constraint(diffusivity.reshape(PLANES, CELLS, LANES), pltpu.HBM),
        rotor_step,
    )
    return result.reshape(1, FIELDS, PLANES, CELLS, LANES)


def solution(mesh):
    return jax.shard_map(
        body,
        mesh=mesh,
        in_specs=(P("ax", None, None, "az", "rad"), P("ax", None, "az", "rad"), P()),
        out_specs=P("ax", None, None, "az", "rad"),
        check_vma=False,
    )
```

```python
import functools
import math

import jax
import jax.numpy as jnp
from jax import lax
from jax.experimental import pallas as pl
from jax.experimental.pallas import tpu as pltpu
from jax.sharding import PartitionSpec as P

CYCLE = 1536
MODES = 512
FIELDS = 6
PLANES = 32
ROWS = FIELDS * PLANES
CELLS = 24
LANES = 128
RING = 64
COLS = 16
FAR = COLS // 2
NEAR = 4
PARTS = 3
GROUP = 8
MESH = pl.DeviceIdType.MESH
F32 = jnp.float32
BF16 = jnp.bfloat16


def iota(shape, dim):
    return lax.broadcasted_iota(jnp.int32, shape, dim)


def wrapped(product):
    left = product - jnp.floor(product * (1.0 / CYCLE)) * float(CYCLE)
    left = jnp.where(left < 0.0, left + float(CYCLE), left)
    return jnp.where(left >= float(CYCLE), left - float(CYCLE), left)


def cos_sin(cells):
    quarter = jnp.floor(cells * (4.0 / CYCLE) + 0.5)
    t = (cells - quarter * (CYCLE / 4.0)) * (2.0 * math.pi / CYCLE)
    u = t * t
    sine = t * (1.0 + u * (-1.0 / 6 + u * (1.0 / 120 + u * (-1.0 / 5040 + u * (1.0 / 362880)))))
    cosine = 1.0 + u * (-0.5 + u * (1.0 / 24 + u * (-1.0 / 720 + u * (1.0 / 40320 - u * (1.0 / 3628800)))))
    odd = (quarter == 1.0) | (quarter == 3.0)
    c = jnp.where(odd, sine, cosine)
    s = jnp.where(odd, cosine, sine)
    c = jnp.where((quarter == 1.0) | (quarter == 2.0), -c, c)
    s = jnp.where((quarter == 2.0) | (quarter == 3.0), -s, s)
    return c, s


def kernel(
    state_hbm,
    diffusivity_hbm,
    rotor_step,
    base,
    carried,
    cycles,
    rebuilt,
    forward,
    back,
    spun,
    phase,
    fine,
    coarse,
    edge_rows,
    near_rows,
    near_rows32,
    edge_cols,
    near_cols,
    near_cols_t,
    face_x,
    face,
    send1,
    recv1,
    send2,
    recv2,
    send_h,
    recv_h,
    state,
    diffusivity,
    load,
    known_below,
    known_above,
):
    az, rad, ax = lax.axis_index("az"), lax.axis_index("rad"), lax.axis_index("ax")
    x, z = az // COLS, lax.rem(az, COLS)
    az_up, az_down = lax.rem(az + 1, RING), lax.rem(az + RING - 1, RING)
    rad_up, rad_down = lax.rem(rad + 1, 4), lax.rem(rad + 3, 4)

    z_up, z_down = lax.rem(z + 1, COLS), lax.rem(z + COLS - 1, COLS)
    loads = [
        pltpu.make_async_copy(state_hbm, state, load.at[0]),
        pltpu.make_async_copy(diffusivity_hbm, diffusivity, load.at[1]),
    ]
    for copy in loads:
        copy.start()

    def signal(semaphore, *device):
        pl.semaphore_signal(semaphore, inc=1, device_id=device, device_id_type=MESH)

    barrier = pltpu.get_barrier_semaphore()
    for turn in range(4):
        run = lax.rem(x + turn, 4) * COLS
        for side in (ax, 1 - ax):
            signal(barrier, run + z_up, rad, side)
            signal(barrier, run + z_down, rad, side)
        signal(barrier, run + z, rad, 1 - ax)
        if turn:
            signal(barrier, run + z, rad, ax)
    signal(barrier, az, rad_up, ax)
    signal(barrier, az, rad_down, ax)
    pl.semaphore_wait(barrier, 25)
    signal(known_below.at[2], x * COLS + z_up, rad, ax)
    signal(known_above.at[2], x * COLS + z_down, rad, ax)
    for copy in loads:
        copy.wait()

    def place(turn, dz):
        return lax.rem(x + turn, 4) * COLS + lax.rem(z + dz, COLS)

    def send_plane(first, count, dz):
        def send(k, carry):
            part, j = first + k // 4, place(lax.rem(k, 4), dz)
            pltpu.make_async_remote_copy(
                src_ref=state.at[part * RING + j],
                dst_ref=cycles.at[part, az],
                send_sem=send1.at[part],
                recv_sem=recv1.at[part],
                device_id=(j, rad, 1 - ax),
                device_id_type=MESH,
            ).start()
            return carry

        lax.fori_loop(0, 4 * count, send, 0)

    def send_both(first, count, far):
        send_plane(first, count, far)
        send_plane(first, count, COLS - far)

    send_plane(0, PARTS, 0)
    send_both(0, PARTS, 1)

    def reach(far, carry, count):
        pl.semaphore_wait(known_below.at[far], 1)
        signal(known_below.at[far + 1], x * COLS + z_up, rad, ax)
        pl.semaphore_wait(known_above.at[far], 1)

        @pl.when(far < FAR - 1)
        def _():
            signal(known_above.at[far + 1], x * COLS + z_down, rad, ax)

        send_both(0, count, far)
        return carry

    lax.fori_loop(2, NEAR + 1, functools.partial(reach, count=PARTS), 0)
    lax.fori_loop(NEAR + 1, FAR, functools.partial(reach, count=1), 0)
    pl.semaphore_wait(known_below.at[FAR], 1)
    send_plane(0, PARTS, FAR)

    def send_rest(i, carry):
        send_both(1 + i // (FAR - 1 - NEAR), 1, FAR - 1 - lax.rem(i, FAR - 1 - NEAR))
        return carry

    lax.fori_loop(0, (PARTS - 1) * (FAR - 1 - NEAR), send_rest, 0)

    def edges(ref, i, slot, acc):
        block = ref[pl.ds(pl.multiple_of(i * 16, 16), 16)]
        wide = block.astype(F32)
        rows = pl.ds(pl.multiple_of(slot * 16, 16), 16)
        edge_rows[0, rows, :] = wide[:, 0, :].astype(BF16)
        edge_rows[1, rows, :] = wide[:, CELLS - 1, :].astype(BF16)
        row, lane = iota((32, LANES), 0), iota((32, LANES), 1)
        pick = ((row == slot) & (lane == 0)) | ((row == slot + 16) & (lane == LANES - 1))
        return acc + lax.dot_general(
            jnp.where(pick, 1.0, 0.0).astype(BF16),
            block.reshape(16 * CELLS, LANES),
            (((1,), (1,)), ((), ())),
            preferred_element_type=F32,
        )

    acc = jnp.zeros((32, 16 * CELLS), F32)
    acc = lax.fori_loop(0, ROWS // 16, lambda i, a: edges(state, i, i, a), acc)
    acc = lax.fori_loop(0, PLANES // 16, lambda i, a: edges(diffusivity, i, i + ROWS // 16, a), acc)
    edge_cols[0] = acc[:16].astype(BF16)
    edge_cols[1] = acc[16:].astype(BF16)

    def halo(n, src, dst, target):
        return pltpu.make_async_remote_copy(
            src_ref=src, dst_ref=dst, send_sem=send_h.at[n], recv_sem=recv_h.at[n],
            device_id=target, device_id_type=MESH,
        )

    halos = [
        halo(0, edge_rows.at[1], near_rows.at[0], (az_up, rad, ax)),
        halo(1, edge_rows.at[0], near_rows.at[1], (az_down, rad, ax)),
        halo(2, edge_cols.at[1], near_cols.at[0], (az, rad_up, ax)),
        halo(3, edge_cols.at[0], near_cols.at[1], (az, rad_down, ax)),
    ]
    for copy in halos:
        copy.start()

    def grid(first, rows, columns):
        a = iota((rows, columns), 0).astype(F32)
        b = iota((rows, columns), 1).astype(F32)
        return cos_sin(wrapped(first * a * b))

    fine[0], fine[1] = grid(1.0, 16, CYCLE)
    coarse[0], coarse[1] = grid(16.0, MODES // 16, CYCLE)

    def forward_rows(i, carry):
        c0, s0 = fine[0], fine[1]
        c1, s1 = coarse[0, pl.ds(i, 1), :], coarse[1, pl.ds(i, 1), :]
        forward[pl.ds(pl.multiple_of(i * 16, 16), 16), :] = (c1 * c0 - s1 * s0).astype(BF16)
        forward[pl.ds(pl.multiple_of(MODES + i * 16, 16), 16), :] = (s1 * c0 + c1 * s0).astype(BF16)
        return carry

    lax.fori_loop(0, MODES // 16, forward_rows, 0)

    weight_k = jnp.where(iota((16, MODES), 1) == 0, 1.0, 2.0).astype(F32) / CYCLE
    fine[0, :, :MODES] = fine[0, :, :MODES] * weight_k
    fine[1, :, :MODES] = fine[1, :, :MODES] * weight_k
    c, s = grid(16.0, CYCLE // 16, MODES)
    for n in range(3):
        coarse[0, :, n * MODES : (n + 1) * MODES] = c[n * 32 : (n + 1) * 32]
        coarse[1, :, n * MODES : (n + 1) * MODES] = s[n * 32 : (n + 1) * 32]
    for n in range(3):

        def back_rows(i, carry, n=n):
            c0, s0 = fine[0, :, :MODES], fine[1, :, :MODES]
            c1 = coarse[0, pl.ds(i, 1), n * MODES : (n + 1) * MODES]
            s1 = coarse[1, pl.ds(i, 1), n * MODES : (n + 1) * MODES]
            rows = pl.ds(pl.multiple_of((n * 32 + i) * 16, 16), 16)
            back[rows, :MODES] = (c1 * c0 - s1 * s0).astype(BF16)
            back[rows, MODES:] = (s1 * c0 + c1 * s0).astype(BF16)
            return carry

        lax.fori_loop(0, 32, back_rows, 0)

    shift = ((2 * ax - 1) * rotor_step[0]).astype(F32)
    phase[0], phase[1] = cos_sin(wrapped(iota((MODES, LANES), 0).astype(F32) * shift))

    def transform(part):
        pltpu.make_async_copy(cycles.at[part], cycles.at[part], recv1.at[part]).wait()
        step = MODES // 2

        def ahead(i, carry):
            rows = pl.ds(pl.multiple_of(i * step, step), step)
            sine_rows = pl.ds(pl.multiple_of(MODES + i * step, step), step)
            cells = cycles[part].reshape(CYCLE, LANES)
            c = jnp.dot(forward[rows, :], cells, preferred_element_type=F32)
            d = jnp.dot(forward[sine_rows, :], cells, preferred_element_type=F32)
            cos_p, sin_p = phase[0, rows, :], phase[1, rows, :]
            spun[rows, :] = (c * cos_p - d * sin_p).astype(BF16)
            spun[sine_rows, :] = (c * sin_p + d * cos_p).astype(BF16)
            return carry

        lax.fori_loop(0, 2, ahead, 0)

        def astern(i, carry):
            rows = pl.ds(pl.multiple_of(i * (CYCLE // 4), CYCLE // 4), CYCLE // 4)
            cells = jnp.dot(back[rows, :], spun[...], preferred_element_type=F32).astype(BF16)
            rebuilt[part, pl.ds(i * COLS, COLS)] = cells.reshape(COLS, CELLS, LANES)
            return carry

        lax.fori_loop(0, 4, astern, 0)
        pltpu.make_async_copy(rebuilt.at[part, az], carried.at[part, az], recv2.at[part]).start()

        def send(k, carry):
            m = COLS - 1 - k // 4
            far = (m + 1) // 2
            j = place(lax.rem(k, 4), jnp.where(lax.rem(m, 2) == 1, far, COLS - far))
            pltpu.make_async_remote_copy(
                src_ref=rebuilt.at[part, j],
                dst_ref=carried.at[part, az],
                send_sem=send2.at[part],
                recv_sem=recv2.at[part],
                device_id=(j, rad, ax),
                device_id_type=MESH,
            ).start()
            return carry

        lax.fori_loop(0, RING - 4, send, 0)
        lax.fori_loop(RING - 3, RING, send, 0)

    lane = iota((GROUP, CELLS, LANES), 2)
    cell = iota((GROUP, CELLS, LANES), 1)

    def around(ref, i, slot, last):
        here = ref[pl.ds(i * GROUP, GROUP)].astype(F32)
        below = ref[pl.ds(jnp.maximum(i * GROUP - 1, 0), 1)].astype(F32)
        above = ref[pl.ds(jnp.minimum(i * GROUP + GROUP, last), 1)].astype(F32)
        plane_down = jnp.concatenate([below, here[:-1]], axis=0)
        plane_up = jnp.concatenate([here[1:], above], axis=0)
        rows = pl.ds(pl.multiple_of(slot * GROUP, GROUP), GROUP)
        cell_down = jnp.where(cell == 0, near_rows32[0, rows, :][:, None, :], pltpu.roll(here, 1, 1))
        cell_up = jnp.where(cell == CELLS - 1, near_rows32[1, rows, :][:, None, :], pltpu.roll(here, CELLS - 1, 1))
        half = lax.rem(slot, 2) * (GROUP * CELLS)
        columns = near_cols_t[pl.ds(pl.multiple_of(half, GROUP * CELLS), GROUP * CELLS), :].astype(BF16)
        pair = slot // 2
        r, l = iota((32, LANES), 0), iota((32, LANES), 1)
        place = ((r == pair) & (l == 0)) | ((r == pair + 16) & (l == LANES - 1))
        beyond = jnp.dot(columns, jnp.where(place, 1.0, 0.0).astype(BF16), preferred_element_type=F32)
        beyond = beyond.reshape(GROUP, CELLS, LANES)
        radius_down = jnp.where(lane == 0, beyond, pltpu.roll(here, 1, 2))
        radius_up = jnp.where(lane == LANES - 1, beyond, pltpu.roll(here, LANES - 1, 2))
        return here, plane_down, plane_up, cell_down, cell_up, radius_down, radius_up

    def side_weight(plane):
        middle = (plane.astype(F32) + 0.5) / PLANES
        return jnp.where(ax == 0, middle, 1.0 - middle)

    def faces(i, carry):
        here, plane_down, plane_up, *others = around(diffusivity, i, ROWS // GROUP + i, PLANES - 1)
        plane = iota((GROUP, CELLS, LANES), 0) + i * GROUP
        planes = pl.ds(i * GROUP, GROUP)
        first, final = plane == 0, plane == PLANES - 1
        down = 0.5 * (here + jnp.where(first, 0.0, plane_down))
        up = 0.5 * (here + jnp.where(final, 0.0, plane_up))
        total = down + up
        face_x[0, planes] = jnp.where(first, 0.0, down)
        face_x[1, planes] = jnp.where(final, 0.0, up)
        for n, other in enumerate(others):
            between = 0.5 * (here + other)
            face[n, planes] = between
            total = total + between
        face[4, planes] = 1.0 - total - side_weight(plane)
        return carry

    def flux(i, carry):
        here, plane_down, plane_up, *others = around(state, i, i, ROWS - 1)
        planes = pl.ds(lax.rem(i, PLANES // GROUP) * GROUP, GROUP)
        total = face[4, planes] * here
        total = total + face_x[0, planes] * plane_down
        total = total + face_x[1, planes] * plane_up
        for n, other in enumerate(others):
            total = total + face[n, planes] * other
        base[pl.ds(i * GROUP, GROUP)] = total
        return carry

    transform(0)

    for copy in halos:
        copy.wait()

    def widen(i, carry):
        rows = pl.ds(pl.multiple_of(i * 16, 16), 16)
        near_rows32[0, rows, :] = near_rows[0, rows, :].astype(F32)
        near_rows32[1, rows, :] = near_rows[1, rows, :].astype(F32)
        return carry

    lax.fori_loop(0, (ROWS + PLANES) // 16, widen, 0)
    low = jnp.where(rad == 0, 0.0, near_cols[0].astype(F32))
    high = jnp.where(rad == 3, 0.0, near_cols[1].astype(F32))
    near_cols_t[...] = jnp.concatenate([low, high], axis=0).T
    lax.fori_loop(0, PLANES // GROUP, faces, 0)
    lax.fori_loop(0, ROWS // GROUP, flux, 0)

    for part in range(1, PARTS):
        transform(part)
    for part in range(PARTS):
        pltpu.make_async_copy(carried.at[part], carried.at[part], recv2.at[part]).wait()
    for part in range(PARTS):
        pltpu.make_async_copy(cycles.at[part], cycles.at[part], send1.at[part]).wait()
        sent = rebuilt.at[part, pl.ds(0, RING - 1)]
        pltpu.make_async_copy(sent, sent, send2.at[part]).wait()


def body(state, diffusivity, rotor_step):
    vmem = pl.BlockSpec(memory_space=pltpu.VMEM)
    hbm = pl.BlockSpec(memory_space=pltpu.HBM)
    block = (PARTS, RING, CELLS, LANES)
    base, carried = pl.pallas_call(
        kernel,
        out_shape=(jax.ShapeDtypeStruct((ROWS, CELLS, LANES), F32), jax.ShapeDtypeStruct(block, BF16)),
        in_specs=[hbm, hbm, pl.BlockSpec(memory_space=pltpu.SMEM)],
        out_specs=(vmem, vmem),
        scratch_shapes=[
            pltpu.VMEM(block, BF16),
            pltpu.VMEM(block, BF16),
            pltpu.VMEM((2 * MODES, CYCLE), BF16),
            pltpu.VMEM((CYCLE, 2 * MODES), BF16),
            pltpu.VMEM((2 * MODES, LANES), BF16),
            pltpu.VMEM((2, MODES, LANES), F32),
            pltpu.VMEM((2, 16, CYCLE), F32),
            pltpu.VMEM((2, MODES // 16, CYCLE), F32),
            pltpu.VMEM((2, ROWS + PLANES, LANES), BF16),
            pltpu.VMEM((2, ROWS + PLANES, LANES), BF16),
            pltpu.VMEM((2, ROWS + PLANES, LANES), F32),
            pltpu.VMEM((2, 16, 16 * CELLS), BF16),
            pltpu.VMEM((2, 16, 16 * CELLS), BF16),
            pltpu.VMEM((16 * CELLS, 32), F32),
            pltpu.VMEM((2, PLANES, CELLS, LANES), F32),
            pltpu.VMEM((5, PLANES, CELLS, LANES), F32),
            pltpu.SemaphoreType.DMA((PARTS,)),
            pltpu.SemaphoreType.DMA((PARTS,)),
            pltpu.SemaphoreType.DMA((PARTS,)),
            pltpu.SemaphoreType.DMA((PARTS,)),
            pltpu.SemaphoreType.DMA((4,)),
            pltpu.SemaphoreType.DMA((4,)),
            pltpu.VMEM((ROWS, CELLS, LANES), BF16),
            pltpu.VMEM((PLANES, CELLS, LANES), BF16),
            pltpu.SemaphoreType.DMA((2,)),
            pltpu.SemaphoreType.REGULAR((FAR + 1,)),
            pltpu.SemaphoreType.REGULAR((FAR + 1,)),
        ],
        compiler_params=pltpu.CompilerParams(
            collective_id=0, has_side_effects=True, vmem_limit_bytes=40 * 1024 * 1024
        ),
    )(
        pltpu.with_memory_space_constraint(state.reshape(ROWS, CELLS, LANES), pltpu.HBM),
        pltpu.with_memory_space_constraint(diffusivity.reshape(PLANES, CELLS, LANES), pltpu.HBM),
        rotor_step,
    )
    middle = (iota((1, PLANES, 1, 1), 1).astype(F32) + 0.5) / PLANES
    weight = jnp.where(lax.axis_index("ax") == 0, middle, 1.0 - middle)
    shape = (FIELDS, PLANES, CELLS, LANES)
    blended = base.reshape(shape) + weight * carried.reshape(shape).astype(F32)
    return blended.astype(BF16)[None]


def solution(mesh):
    return jax.shard_map(
        body,
        mesh=mesh,
        in_specs=(P("ax", None, None, "az", "rad"), P("ax", None, "az", "rad"), P()),
        out_specs=P("ax", None, None, "az", "rad"),
        check_vma=False,
    )
```
